32 devices in a mesh: dp: 4 (over y, core), mp: 8 (over z, x).
Axes of the slice: x: 2, y: 2, z: 4, core: 2. Of those that a mesh axis runs over, the one named last changes fastest.
Arguments:
- embed_table: float32 [131072, 128], P(('dp', 'mp')), may hold values from -4 to 4
- dual_state: float32 [131072, 128], P(('dp', 'mp')), may hold values from -6 to 6
- grad_squares: float32 [131072, 128], P(('dp', 'mp')), may hold values from 0.002 to 0.2
- indices_now: int32 [2048, 16], P('dp', 'mp'), may hold values from 0 to 131071, as said below
- indices_next: int32 [2048, 16], P('dp', 'mp'), may hold values from 0 to 131071, as said below
- click_labels: int32 [2048], P('dp'), may hold values 0 or 1
- first_weight: bfloat16 [2048, 1024], P('mp'), may hold values from -0.5 to 0.5
- first_bias: float32 [1024], replicated, may hold values from -6 to 6
- output_weight: float32 [1024], replicated, may hold values from -1 to 1
Outputs:
- updated_table: float32 [131072, 128], P(('dp', 'mp'))
- updated_dual: float32 [131072, 128], P(('dp', 'mp'))
- updated_squares: float32 [131072, 128], P(('dp', 'mp'))
- next_logits: float32 [2048], P('dp')
The draws below stay inside these ranges and needn't reach their ends.
Inputs may be any that keep to these rules, and one draw needn't show every extreme that they name: `indices_now`: the row r is owned by device r // 4096 of dp+mp. The lookups of one device's block (its 512 samples and 2 fields) name at most 64 rows owned by any one device, counted with repeats, and exactly 64 for some owners in every block. `indices_next`: same law as indices_now: at most 64 lookups of one device's block go to rows of one owner, exactly 64 for some owners in every block.
All inputs are finite; a program needn't handle non-finite values. No bound on the sum of `click_labels` on one device may be relied on, other than what follows from the above.
Results may differ from the reference program's by a relative error of at most 0.015.
Values may be sent and summed in bfloat16 or wider, within the bound.
A program may use at most 64 MiB of HBM per device.

```python
import math
import jax
import jax.numpy as jnp
from jax import lax

ROW_WIDTH = 128
HIDDEN_UNITS = 1024
FIELD_DEV = 2
SAMP_DP = 512
ROWS_DEV = 4096
FIELDS = 16
SAMPLES = 2048
ROWS = 131072
CAPACITY = 64
N_DP = 4
N_MP = 8
DEVICES = 32


def owner_rows(key):
    looked = SAMP_DP * FIELD_DEV
    hot_count = DEVICES // 4
    hot_part = hot_count * CAPACITY
    order = jax.random.permutation(jax.random.fold_in(key, 11), DEVICES).astype(jnp.int32)
    position = jnp.arange(looked, dtype=jnp.int32)
    hot_pick = order[jnp.minimum(position // CAPACITY, hot_count - 1)]
    cold_pick = order[hot_count + jnp.maximum(position - hot_part, 0) % (DEVICES - hot_count)]
    owner_line = jnp.where(position < hot_part, hot_pick, cold_pick)
    block_keys = jax.random.split(jax.random.fold_in(key, 12), DEVICES)

    def shuffle_block(single_key):
        return jax.random.permutation(single_key, looked).astype(jnp.int32)
    shuffles = jax.vmap(shuffle_block)(block_keys)
    owners = owner_line[shuffles]
    local_rows = jax.random.randint(jax.random.fold_in(key, 13), (DEVICES, looked), 0, ROWS_DEV, dtype=jnp.int32)
    flat_rows = owners * ROWS_DEV + local_rows
    shaped = flat_rows.reshape(N_DP, N_MP, SAMP_DP, FIELD_DEV)
    return jnp.transpose(shaped, (0, 2, 1, 3)).reshape(SAMP_DP * N_DP, FIELD_DEV * N_MP)


def draw_indices_now(key, part):
    key = jax.random.fold_in(key, 1)
    return owner_rows(key)


def draw_indices_next(key, part):
    key = jax.random.fold_in(key, 2)
    return owner_rows(key)


def touch_ends(drawn, rng, least, largest):
    shape = drawn.shape
    spot = [jax.random.randint(jax.random.fold_in(rng, axis), (), 0, shape[axis]) for axis in range(len(shape))]
    drawn = drawn.at[tuple(spot)].set(least)
    longest = shape.index(max(shape))
    spot[longest] = (spot[longest] + 1) % shape[longest]
    return drawn.at[tuple(spot)].set(largest)


def steps_of(rng, extent, shards, least, high):
    def one(dim, parts):
        heights = jax.random.uniform(jax.random.fold_in(jax.random.fold_in(rng, 6), dim), (parts,), jnp.float32, least / len(shards), high / len(shards))
        return jnp.repeat(jnp.exp(heights), extent[dim] // parts).reshape((-1,) + (1,) * (len(extent) - dim - 1))

    factor_of = one(*shards[0])
    for cut in shards[1:]:
        factor_of = factor_of * one(*cut)
    return factor_of


def bell_draw(rng, extent, deviation, bound, cuts=(), kind=jnp.bfloat16):
    values = deviation * jax.random.normal(rng, extent, jnp.float32)
    if cuts:
        values = values * steps_of(rng, extent, cuts, -0.22, 0.18)
    return jnp.clip(values, -bound, bound).astype(kind)


def setup_inputs(seed: int = 0) -> dict:
    key_of = jax.random.split(jax.random.key(seed), 10)
    return {
        "embed_table": bell_draw(key_of[0], (ROWS, ROW_WIDTH), 0.3, 4.0, ((0, 32),), jnp.float32),
        "dual_state": bell_draw(key_of[1], (ROWS, ROW_WIDTH), 0.4, 6.0, ((0, 32),), jnp.float32),
        "grad_squares": jnp.clip(jnp.exp(math.log(0.2) - 4.6051702 * jax.random.uniform(key_of[2], (ROWS, ROW_WIDTH), jnp.float32) ** steps_of(key_of[2], (ROWS, ROW_WIDTH), ((0, 32),), -0.2, 0.2)), 0.002, 0.2),
        "indices_now": draw_indices_now(jax.random.fold_in(key_of[9], 71), 0),
        "indices_next": draw_indices_next(jax.random.fold_in(key_of[9], 71), 0),
        "click_labels": touch_ends((jax.random.randint(key_of[5], (SAMPLES,), 0, 2) < 1).astype(jnp.int32), jax.random.fold_in(key_of[5], 1), 0, 1),
        "first_weight": bell_draw(key_of[6], (FIELDS * ROW_WIDTH, HIDDEN_UNITS), (FIELDS * ROW_WIDTH // 16) ** -0.5, 0.5, ((0, 8),)),
        "first_bias": bell_draw(key_of[7], (HIDDEN_UNITS,), 1.0, 6.0, (), jnp.float32),
        "output_weight": bell_draw(key_of[8], (HIDDEN_UNITS,), (HIDDEN_UNITS // 32) ** -0.5, 1.0, (), jnp.float32),
    }


learn_alpha = 1.0
learn_beta = 1.0
lasso_weight = 0.1
ridge_weight = 0.1

def forward_pre(looked, first_weight, first_bias):
    samples = looked.shape[0]
    blocks = looked.reshape(samples, N_MP, FIELD_DEV * ROW_WIDTH)
    weights = first_weight.reshape(N_MP, FIELD_DEV * ROW_WIDTH, HIDDEN_UNITS)

    def accumulate(running, position):
        term = jnp.dot(blocks[:, position], weights[position], preferred_element_type=jnp.float32)
        rounded = lax.optimization_barrier(term.astype(jnp.bfloat16))
        return (running + rounded.astype(jnp.float32), None)
    start = jnp.zeros((samples, HIDDEN_UNITS), jnp.float32)
    summed_pre, unused = lax.scan(accumulate, start, jnp.arange(N_MP, dtype=jnp.int32))
    return summed_pre + first_bias[None, :]

def logits_of(pre, output_weight):
    return jnp.dot(jax.nn.silu(pre), output_weight, precision=lax.Precision.HIGHEST)

def slope_of(pre, logits, labels, output_weight):
    error_term = jax.nn.sigmoid(logits) - labels.astype(jnp.float32)
    gate_value = jax.nn.sigmoid(pre)
    derivative = gate_value * (1.0 + pre * (1.0 - gate_value))
    return (error_term[:, None] * output_weight[None, :] * derivative).astype(jnp.bfloat16)

def proximal_update(weights, dual, squares, grads, touched):
    new_squares = squares + grads * grads
    sigma_term = (jnp.sqrt(new_squares) - jnp.sqrt(squares)) / learn_alpha
    new_dual = dual + grads - sigma_term * weights
    shrunk = new_dual - jnp.sign(new_dual) * lasso_weight
    scale_term = (learn_beta + jnp.sqrt(new_squares)) / learn_alpha + ridge_weight
    new_weights = jnp.where(jnp.abs(new_dual) <= lasso_weight, jnp.zeros_like(shrunk), -shrunk / scale_term)
    keep = touched[:, None]
    return (jnp.where(keep, new_weights, weights), jnp.where(keep, new_dual, dual), jnp.where(keep, new_squares, squares))

def reference(embed_table, dual_state, grad_squares, indices_now, indices_next, click_labels, first_weight, first_bias, output_weight):
    samples = indices_now.shape[0]
    looked_now = embed_table[indices_now].astype(jnp.bfloat16).reshape(samples, FIELDS * ROW_WIDTH)
    pre_now = forward_pre(looked_now, first_weight, first_bias)
    logits_now = logits_of(pre_now, output_weight)
    slope = slope_of(pre_now, logits_now, click_labels, output_weight)
    row_grads = lax.dot_general(slope, first_weight, (((1,), (1,)), ((), ())), preferred_element_type=jnp.float32)
    flat_ids = indices_now.reshape(-1)
    summed = jnp.zeros(embed_table.shape, jnp.float32).at[flat_ids].add(row_grads.reshape(-1, ROW_WIDTH))
    hits = jnp.zeros((embed_table.shape[0],), jnp.int32).at[flat_ids].add(jnp.ones(flat_ids.shape, jnp.int32))
    updated_table, updated_dual, updated_squares = proximal_update(embed_table, dual_state, grad_squares, summed, hits > 0)
    looked_next = updated_table[indices_next].astype(jnp.bfloat16).reshape(samples, FIELDS * ROW_WIDTH)
    pre_next = forward_pre(looked_next, first_weight, first_bias)
    next_logits = logits_of(pre_next, output_weight)
    return (updated_table, updated_dual, updated_squares, next_logits)
```

```python
import functools

import jax
import jax.numpy as jnp
from jax import lax
from jax.experimental import pallas as pl
from jax.experimental.pallas import tpu as pltpu
from jax.sharding import PartitionSpec as P

MESH = pl.DeviceIdType.MESH
LASSO = 0.1
RIDGE = 0.1
BETA = 1.0
F32 = jnp.float32
BF16 = jnp.bfloat16


def onehot(mask):
    return jnp.where(mask, 1.0, 0.0).astype(BF16)


def mm(a, b):
    return jnp.dot(a, b, preferred_element_type=F32)


def log2(v):
    assert v & (v - 1) == 0
    return v.bit_length() - 1


def train(
    D, M, C, GROUP,
    cols, labels, bias, wout, table_h, dual_h, sq_h, w_h,
    tab_o, dual_o, sq_o, lg_o,
    tab, dual, sq, tabh, newh, w,
    rowscr, req_send, asked, idcol, idrow,
    send_now, recv_now, send_grad, recv_grad, send_next, recv_next,
    look, part_send, part_recv, slope, rg, rg_out, lg_all,
    lsem, osem, ssem, rsem,
):
    S = cols.shape[0]
    F = cols.shape[1] // 2
    R, W = tab.shape
    H = bias.shape[1]
    FW = F * W
    half = S // 2
    nb = M // 2
    B = half // nb
    slots = D * C
    rsh, csh = log2(R), log2(C)
    dp, mp = lax.axis_index("dp"), lax.axis_index("mp")
    me = dp * M + mp
    h = lax.rem(mp, 2)
    myb = lax.div(mp, 2)
    partner = (dp, mp + 1 - 2 * h)

    def device(p):
        return (lax.div(p, M), lax.rem(p, M))

    bar = pltpu.get_barrier_semaphore()

    def greet(k, c):
        pl.semaphore_signal(
            bar, inc=1, device_id=device(lax.rem(me + k, D)), device_id_type=MESH
        )
        return c

    lax.fori_loop(1, D, greet, 0)

    loads = [
        pltpu.make_async_copy(table_h, tab, lsem.at[0]),
        pltpu.make_async_copy(w_h, w.at[0], lsem.at[1]),
        pltpu.make_async_copy(dual_h, dual, lsem.at[2]),
        pltpu.make_async_copy(sq_h, sq, lsem.at[3]),
    ]
    for load in loads:
        load.start()

    def remote(src, dst, n, to):
        return pltpu.make_async_remote_copy(
            src_ref=src, dst_ref=dst, send_sem=ssem.at[n], recv_sem=rsem.at[n],
            device_id=to, device_id_type=MESH,
        )

    lane = lax.broadcasted_iota(jnp.int32, (S, 128), 1)
    tri = onehot(
        lax.broadcasted_iota(jnp.int32, (S, S), 0)
        > lax.broadcasted_iota(jnp.int32, (S, S), 1)
    )
    owners, members = [], []
    for q in range(2 * F):
        owner = (lax.shift_right_logical(cols[:, q : q + 1], rsh) - me) & (D - 1)
        owners.append(owner)
        members.append(jnp.where(owner == lane, 1.0, 0.0))
    counts = mm(tri, jnp.concatenate(members, axis=1).astype(BF16))
    ranks = []
    packed = jnp.zeros((S, 128), F32)
    for q in range(2 * F):
        count = counts[:, q * 128 : (q + 1) * 128]
        for before in range((q // F) * F, q):
            count = count + jnp.sum(members[before], axis=0, keepdims=True)
        rank = jnp.sum(count * members[q], axis=1, keepdims=True).astype(jnp.int32)
        ranks.append(rank)
        packed = jnp.where(lane == q, (owners[q] * C + rank).astype(F32), packed)
    rowscr[...] = packed.T[0:8, :].astype(jnp.int32)
    total = jnp.zeros((D, 256), F32)
    owner_iota = lax.broadcasted_iota(jnp.int32, (D, S), 0)
    for q in range(2 * F):
        owner_row = lax.shift_right_logical(rowscr[q : q + 1, :], csh)
        which = ranks[q] + (q // F) * C == lane
        value = (cols[:, q : q + 1] & (R - 1)) + 1
        high = jnp.where(which, lax.shift_right_logical(value, 6).astype(F32), 0.0)
        low = jnp.where(which, (value & 63).astype(F32), 0.0)
        total += mm(
            onehot(owner_row == owner_iota),
            jnp.concatenate([high, low], axis=1).astype(BF16),
        )
    request = (total[:, :128] * 64.0 + total[:, 128:]).astype(jnp.int32) - 1
    for r in range(D):
        req_send[r * 8 : (r + 1) * 8, :] = jnp.broadcast_to(request[r : r + 1, :], (8, 128))

    pl.semaphore_wait(bar, D - 1)

    def exchange(rows, send, recv, n, first, last):
        def one(r, c):
            remote(
                send.at[pl.ds(pl.multiple_of(r * rows, rows), rows)],
                recv.at[pl.ds(pl.multiple_of((D - r) * rows, rows), rows)],
                n, device(lax.rem(me + r, D)),
            ).start()
            return c

        lax.fori_loop(first, last, one, 0)

    def arrived(rows, send, recv, n):
        area = pl.ds(rows, (D - 1) * rows)
        return remote(send.at[area], recv.at[area], n, partner)

    exchange(8, req_send, asked, 0, 1, D)
    asked[0:8, :] = req_send[0:8, :]
    loads[1].wait()
    copy_w = remote(w.at[0], w.at[1], 1, partner)
    copy_w.start()
    loads[0].wait()
    tabh[...] = tab[...].astype(BF16)
    copy_req = arrived(8, req_send, asked, 0)
    copy_req.wait_recv()

    asked_t = asked[...].astype(F32).T.astype(jnp.int32)
    for r in range(D):
        for t in range(2):
            idcol[t, r * C : (r + 1) * C, :] = jnp.broadcast_to(
                asked_t[t * C : (t + 1) * C, 8 * r : 8 * r + 1], (C, 128)
            )

    KC = 1024

    def fetch(t, source, send, recv, n):
        def group(g, c):
            rows = pl.ds(pl.multiple_of(g * GROUP, GROUP), GROUP)
            ids = idcol[t, rows, 0:1]
            acc = jnp.zeros((GROUP, W), F32)
            for k in range(R // KC):
                pick = onehot(
                    ids == lax.broadcasted_iota(jnp.int32, (GROUP, KC), 1) + k * KC
                )
                acc = acc + mm(pick, source[k * KC : (k + 1) * KC, :])
            send[rows, :] = acc.astype(BF16)
            peers = GROUP // C
            exchange(C, send, recv, n, jnp.maximum(g * peers, 1), (g + 1) * peers)
            return c

        lax.fori_loop(0, slots // GROUP, group, 0)
        recv[0:C, :] = send[0:C, :]

    def forward(t, recv, n):
        for f in range(F):
            owner_rank = jnp.broadcast_to(slot_col[t * F + f], (S, slots))
            pick = onehot(owner_rank == lax.broadcasted_iota(jnp.int32, (S, slots), 1))
            got = mm(pick, recv[...]).astype(BF16)
            look[t, 0, :, f * W : (f + 1) * W] = got[:half]
            look[t, 1, :, f * W : (f + 1) * W] = got[half:]
        swap = remote(look.at[t, 1 - h], look.at[t, 2], n, partner)
        swap.start()
        if t == 0:
            copy_w.wait_recv()
        swap.wait_recv()

        def step(i, c):
            k = i + 1
            b = lax.rem(myb + k, nb)
            rows = pl.ds(pl.multiple_of(b * B, B), B)
            value = mm(look[t, h, rows, :], w[0]) + mm(look[t, 2, rows, :], w[1])
            part_send[t, k] = value.astype(BF16)
            remote(
                part_send.at[t, k], part_recv.at[t, nb - k], n + 1, (dp, 2 * b + h)
            ).start()
            return c

        lax.fori_loop(0, nb - 1, step, 0)
        rows = pl.ds(pl.multiple_of(myb * B, B), B)
        pre = mm(look[t, h, rows, :], w[0]) + mm(look[t, 2, rows, :], w[1])
        pre = pre + bias[...]
        moved = remote(
            part_send.at[t, pl.ds(1, nb - 1)], part_recv.at[t, pl.ds(1, nb - 1)],
            n + 1, partner,
        )
        moved.wait_recv()
        for k in range(1, nb):
            pre = pre + part_recv[t, k].astype(F32)
        gate = jax.nn.sigmoid(pre)
        logits = jnp.sum(pre * gate * wout[...], axis=1, keepdims=True)
        return pre, gate, logits, [swap, moved]

    slot_col = [owners[q] * C + ranks[q] for q in range(2 * F)]
    fetch(0, tabh, send_now, recv_now, 2)
    for blk in range(slots // 128):
        flipped = idcol[0, blk * 128 : (blk + 1) * 128, :].astype(F32).T
        idrow[:, blk * 128 : (blk + 1) * 128] = flipped[0:8, :].astype(jnp.int32)
    copy_now = arrived(C, send_now, recv_now, 2)
    copy_now.wait_recv()
    pre, gate, logits, sent_now = forward(0, recv_now, 3)
    mine = pl.ds(pl.multiple_of(h * half + myb * B, B), B)
    error = jax.nn.sigmoid(logits) - labels[mine, :].astype(F32)
    slope[0] = (error * wout[...] * (gate * (1.0 + pre * (1.0 - gate)))).astype(BF16)

    def spread(k, c):
        remote(
            slope.at[0], slope.at[nb - k], 5, (dp, 2 * lax.rem(myb + k, nb) + h)
        ).start()
        return c

    lax.fori_loop(1, nb, spread, 0)

    def back(k):
        rows = pl.ds(pl.multiple_of(lax.rem(myb + k, nb) * B, B), B)
        for side in range(2):
            value = lax.dot_general(
                slope[k], w[side], (((1,), (1,)), ((), ())), preferred_element_type=F32
            ).astype(BF16)
            if side == 0:
                rg[h, rows, :] = value
            else:
                rg_out[rows, :] = value

    back(0)
    copy_slope = remote(slope.at[pl.ds(1, nb - 1)], slope.at[pl.ds(1, nb - 1)], 5, partner)
    copy_slope.wait_recv()
    for k in range(1, nb):
        back(k)
    swap_grad = remote(rg_out, rg.at[h], 6, partner)
    swap_grad.start()
    swap_grad.wait_recv()

    def give(g, c):
        rows = pl.ds(pl.multiple_of(g * GROUP, GROUP), GROUP)
        acc = jnp.zeros((GROUP, W), F32)
        spot = lax.broadcasted_iota(jnp.int32, (GROUP, half), 0) + g * GROUP
        for f in range(F):
            for s in range(2):
                pick = onehot(rowscr[f : f + 1, s * half : (s + 1) * half] == spot)
                acc = acc + mm(pick, rg[s, :, f * W : (f + 1) * W])
        send_grad[rows, :] = acc.astype(BF16)
        peers = GROUP // C
        exchange(C, send_grad, recv_grad, 7, jnp.maximum(g * peers, 1), (g + 1) * peers)
        return c

    lax.fori_loop(0, slots // GROUP, give, 0)
    recv_grad[0:C, :] = send_grad[0:C, :]
    loads[2].wait()
    loads[3].wait()
    copy_grad = arrived(C, send_grad, recv_grad, 7)
    copy_grad.wait_recv()

    RC = 256
    gathered = jnp.concatenate([recv_grad[...], jnp.ones((slots, 128), BF16)], axis=1)

    def update(i, c):
        rows = pl.ds(pl.multiple_of(i * RC, RC), RC)
        spot = lax.broadcasted_iota(jnp.int32, (RC, slots), 0) + i * RC
        both = mm(onehot(idrow[0:1, :] == spot), gathered)
        g, keep = both[:, :W], both[:, W:] > 0.5
        old_w, old_d, old_s = tab[rows, :], dual[rows, :], sq[rows, :]
        new_s = old_s + g * g
        root = jnp.sqrt(new_s)
        new_d = old_d + g - (root - jnp.sqrt(old_s)) * old_w
        shrunk = jnp.where(new_d > 0.0, new_d - LASSO, new_d + LASSO)
        new_w = jnp.where(
            jnp.abs(new_d) <= LASSO, 0.0, -shrunk / ((BETA + root) + RIDGE)
        )
        new_w = jnp.where(keep, new_w, old_w)
        tab[rows, :] = new_w
        newh[rows, :] = new_w.astype(BF16)
        dual[rows, :] = jnp.where(keep, new_d, old_d)
        sq[rows, :] = jnp.where(keep, new_s, old_s)
        return c

    lax.fori_loop(0, R // RC, update, 0)
    stores = [
        pltpu.make_async_copy(tab, tab_o, osem.at[0]),
        pltpu.make_async_copy(dual, dual_o, osem.at[1]),
        pltpu.make_async_copy(sq, sq_o, osem.at[2]),
    ]
    for store in stores:
        store.start()

    fetch(1, newh, send_next, recv_next, 8)
    copy_next = arrived(C, send_next, recv_next, 8)
    copy_next.wait_recv()
    pre, gate, logits, sent_next = forward(1, recv_next, 9)
    wide = jnp.broadcast_to(logits, (B, 128))
    if B < 128:
        wide = jnp.concatenate([wide, jnp.zeros((128 - B, 128), F32)], axis=0)
    lg_all[mp] = wide.T[0:8, :]

    def tell(k, c):
        remote(lg_all.at[mp], lg_all.at[mp], 11, (dp, lax.rem(mp + k, M))).start()
        return c

    lax.fori_loop(1, M, tell, 0)
    for copy in (copy_req, copy_w, copy_now, *sent_now, copy_slope, swap_grad, copy_grad,
                 copy_next, *sent_next):
        copy.wait_send()
    for store in stores:
        store.wait()
    told = remote(lg_all.at[pl.ds(0, M - 1)], lg_all.at[pl.ds(0, M - 1)], 11, partner)
    told.wait_send()
    told.wait_recv()
    lg_o[...] = lg_all[...]


def shards(table, dual, squares, now, later, labels, weight, bias, wout):
    M = lax.axis_size("mp")
    D = lax.axis_size("dp") * M
    R, W = table.shape
    S, F = now.shape
    H = weight.shape[1]
    C = 2 * now.size // D
    slots = D * C
    GROUP = 512
    nb = M // 2
    B = S // M
    vm = pl.BlockSpec(memory_space=pltpu.VMEM)
    hb = pl.BlockSpec(memory_space=pl.ANY)
    rows_buf = pltpu.VMEM((slots, W), BF16)
    big = pltpu.VMEM((R, W), F32)
    state = jax.ShapeDtypeStruct((R, W), F32)
    outs = pl.pallas_call(
        functools.partial(train, D, M, C, GROUP),
        out_shape=(state, state, state, jax.ShapeDtypeStruct((M, 8, 128), F32)),
        in_specs=[vm, vm, vm, vm, hb, hb, hb, hb],
        out_specs=(hb, hb, hb, vm),
        scratch_shapes=[
            big, big, big,
            pltpu.VMEM((R, W), BF16), pltpu.VMEM((R, W), BF16),
            pltpu.VMEM((2, F * W, H), BF16),
            pltpu.VMEM((8, S), jnp.int32),
            pltpu.VMEM((D * 8, 128), jnp.int32), pltpu.VMEM((D * 8, 128), jnp.int32),
            pltpu.VMEM((2, slots, 128), jnp.int32), pltpu.VMEM((8, slots), jnp.int32),
            rows_buf, rows_buf, rows_buf, rows_buf, rows_buf, rows_buf,
            pltpu.VMEM((2, 3, S // 2, F * W), BF16),
            pltpu.VMEM((2, nb, B, H), BF16), pltpu.VMEM((2, nb, B, H), BF16),
            pltpu.VMEM((nb, B, H), BF16),
            pltpu.VMEM((2, S // 2, F * W), BF16), pltpu.VMEM((S // 2, F * W), BF16),
            pltpu.VMEM((M, 8, 128), F32),
            pltpu.SemaphoreType.DMA((4,)), pltpu.SemaphoreType.DMA((3,)),
            pltpu.SemaphoreType.DMA((12,)), pltpu.SemaphoreType.DMA((12,)),
        ],
        compiler_params=pltpu.CompilerParams(
            collective_id=0, has_side_effects=True, vmem_limit_bytes=58 * 1024 * 1024
        ),
    )(
        jnp.concatenate([now, later], axis=1), labels[:, None], bias[None, :],
        wout[None, :], table, dual, squares, weight,
    )
    logits = outs[3][:, 0, :B].reshape(nb, 2, B).transpose(1, 0, 2).reshape(S)
    return outs[0], outs[1], outs[2], logits


def solution(mesh):
    own = P(("dp", "mp"), None)
    placed = (own, own, own, P("dp", "mp"), P("dp", "mp"), P("dp"), P("mp", None), P(), P())
    return jax.shard_map(
        shards, mesh=mesh, in_specs=placed, out_specs=(own, own, own, P("dp")),
        check_vma=False,
    )
```

```python
import functools

import jax
import jax.numpy as jnp
from jax import lax
from jax.experimental import pallas as pl
from jax.experimental.pallas import tpu as pltpu
from jax.sharding import PartitionSpec as P

MESH = pl.DeviceIdType.MESH
LASSO = 0.1
RIDGE = 0.1
BETA = 1.0
TEAM = 4
F32 = jnp.float32
BF16 = jnp.bfloat16


def onehot(mask):
    return jnp.where(mask, 1.0, 0.0).astype(BF16)


def mm(a, b):
    return jnp.dot(a, b, preferred_element_type=F32)


def log2(v):
    assert v & (v - 1) == 0
    return v.bit_length() - 1


def train(
    D, M, C, GROUP,
    now_t, later_t, labels_t, bias, wout, table_h, dual_h, sq_h, w_h,
    tab_o, dual_o, sq_o, lg_o,
    tab, dual, sq, tabh, newh, w, scatter,
    colscr, slotcol, rowscr, req_send, asked, idcol, idrow,
    send_now, recv_now, send_grad, recv_grad, send_next, recv_next,
    look, look_in, part_send, part_recv, slope, rg, rg_out, lg_col, lg_all,
    lsem, osem, ssem, rsem,
):
    F, S = now_t.shape
    R, W = tab.shape
    H = bias.shape[1]
    FW = F * W
    part = S // TEAM
    nb = M // TEAM
    B = part // nb
    slots = D * C
    rsh, csh = log2(R), log2(C)
    dp, mp = lax.axis_index("dp"), lax.axis_index("mp")
    me = dp * M + mp
    g = lax.rem(mp, TEAM)
    myb = lax.div(mp, TEAM)
    core = lax.rem(dp, 2)
    sibling = (dp + 1 - 2 * core, mp)

    def mate(k):
        return (dp, myb * TEAM + lax.rem(g + k, TEAM))

    def twin(k):
        return (dp, lax.rem(myb + k, nb) * TEAM + g)

    partner = mate(1)

    def device(p):
        return (lax.div(p, M), lax.rem(p, M))

    bar = pltpu.get_barrier_semaphore()

    def greet(k, c):
        pl.semaphore_signal(
            bar, inc=1, device_id=device(lax.rem(me + k, D)), device_id_type=MESH
        )
        return c

    lax.fori_loop(1, D, greet, 0)

    loads = [
        pltpu.make_async_copy(table_h, tab, lsem.at[0]),
        pltpu.make_async_copy(w_h, w.at[0], lsem.at[1]),
        pltpu.make_async_copy(dual_h, dual, lsem.at[2]),
        pltpu.make_async_copy(sq_h, sq, lsem.at[3]),
    ]
    for load in loads:
        load.start()

    def remote(src, dst, n, to):
        return pltpu.make_async_remote_copy(
            src_ref=src, dst_ref=dst, send_sem=ssem.at[n], recv_sem=rsem.at[n],
            device_id=to, device_id_type=MESH,
        )

    lane = lax.broadcasted_iota(jnp.int32, (S, 128), 1)
    tri = onehot(
        lax.broadcasted_iota(jnp.int32, (S, S), 0)
        > lax.broadcasted_iota(jnp.int32, (S, S), 1)
    )
    sub = lax.broadcasted_iota(jnp.int32, (128, S), 0)
    stacked = jnp.zeros((128, S), F32)
    for q in range(2 * F + 1):
        line = labels_t[...] if q == 2 * F else (now_t, later_t)[q // F][q % F : q % F + 1, :]
        stacked = jnp.where(sub == q, line.astype(F32), stacked)
    colscr[...] = stacked.T
    cols = colscr[...].astype(jnp.int32)
    owners, members = [], []
    for q in range(2 * F):
        owner = (lax.shift_right_logical(cols[:, q : q + 1], rsh) - me) & (D - 1)
        owners.append(owner)
        members.append(jnp.where(owner == lane, 1.0, 0.0))
    counts = mm(tri, jnp.concatenate(members, axis=1).astype(BF16))
    ranks = []
    packed = jnp.zeros((S, 128), F32)
    for q in range(2 * F):
        count = counts[:, q * 128 : (q + 1) * 128]
        for before in range((q // F) * F, q):
            count = count + jnp.sum(members[before], axis=0, keepdims=True)
        rank = jnp.sum(count * members[q], axis=1, keepdims=True).astype(jnp.int32)
        ranks.append(rank)
        packed = jnp.where(lane == q, (owners[q] * C + rank).astype(F32), packed)
    slotcol[...] = packed.astype(jnp.int32)
    rowscr[...] = packed.T[0:8, :].astype(jnp.int32)
    total = jnp.zeros((D, 256), F32)
    owner_iota = lax.broadcasted_iota(jnp.int32, (D, S), 0)
    for q in range(2 * F):
        owner_row = lax.shift_right_logical(rowscr[q : q + 1, :], csh)
        which = ranks[q] + (q // F) * C == lane
        value = (cols[:, q : q + 1] & (R - 1)) + 1
        high = jnp.where(which, lax.shift_right_logical(value, 6).astype(F32), 0.0)
        low = jnp.where(which, (value & 63).astype(F32), 0.0)
        total += mm(
            onehot(owner_row == owner_iota),
            jnp.concatenate([high, low], axis=1).astype(BF16),
        )
    request = (total[:, :128] * 64.0 + total[:, 128:]).astype(jnp.int32) - 1
    for r in range(D):
        req_send[r * 8 : (r + 1) * 8, :] = jnp.broadcast_to(request[r : r + 1, :], (8, 128))

    pl.semaphore_wait(bar, D - 1)

    def exchange(rows, send, recv, n, first, last):
        def one(r, c):
            remote(
                send.at[pl.ds(pl.multiple_of(r * rows, rows), rows)],
                recv.at[pl.ds(pl.multiple_of((D - r) * rows, rows), rows)],
                n, device(lax.rem(me + r, D)),
            ).start()
            return c

        lax.fori_loop(first, last, one, 0)

    def arrived(rows, send, recv, n):
        area = pl.ds(rows, (D - 1) * rows)
        return remote(send.at[area], recv.at[area], n, partner)

    exchange(8, req_send, asked, 0, 1, D)
    asked[0:8, :] = req_send[0:8, :]
    loads[1].wait()
    share = pl.ds(pl.multiple_of(core * (FW // 2), FW // 2), FW // 2)
    for k in range(1, TEAM):
        remote(w.at[0, share], w.at[TEAM - k, share], 1, mate(k)).start()
    others = w.at[pl.ds(1, TEAM - 1), share]
    copy_w = remote(others, others, 1, partner)
    pass_w = remote(others, others, 12, sibling)
    loads[0].wait()
    tabh[...] = tab[...].astype(BF16)
    copy_req = arrived(8, req_send, asked, 0)
    copy_req.wait_recv()

    asked_t = asked[...].astype(F32).T.astype(jnp.int32)
    for r in range(D):
        for t in range(2):
            idcol[t, r * C : (r + 1) * C, :] = jnp.broadcast_to(
                asked_t[t * C : (t + 1) * C, 8 * r : 8 * r + 1], (C, 128)
            )

    KC = 1024

    def fetch(t, source, send, recv, n):
        def group(i, c):
            rows = pl.ds(pl.multiple_of(i * GROUP, GROUP), GROUP)
            ids = idcol[t, rows, 0:1]
            acc = jnp.zeros((GROUP, W), F32)
            for k in range(R // KC):
                pick = onehot(
                    ids == lax.broadcasted_iota(jnp.int32, (GROUP, KC), 1) + k * KC
                )
                acc = acc + mm(pick, source[k * KC : (k + 1) * KC, :])
            send[rows, :] = acc.astype(BF16)
            peers = GROUP // C
            exchange(C, send, recv, n, jnp.maximum(i * peers, 1), (i + 1) * peers)
            return c

        lax.fori_loop(0, slots // GROUP, group, 0)
        recv[0:C, :] = send[0:C, :]

    def forward(t, recv, n):
        def look_up(k):
            rows = pl.ds(pl.multiple_of(lax.rem(g + k, TEAM) * part, part), part)
            slot = jnp.concatenate(
                [slotcol[rows, t * F + f : t * F + f + 1] for f in range(F)], axis=0
            )
            pick = onehot(slot == lax.broadcasted_iota(jnp.int32, (F * part, slots), 1))
            got = mm(pick, recv[...]).astype(BF16)
            for f in range(F):
                look[t, k, :, f * W : (f + 1) * W] = got[f * part : (f + 1) * part]

        for k in range(1, TEAM):
            look_up(k)
            remote(look.at[t, k], look_in.at[t, TEAM - k], n, mate(k)).start()
        look_up(0)
        look_in[t, 0] = look[t, 0]
        swap = remote(
            look.at[t, pl.ds(1, TEAM - 1)], look_in.at[t, pl.ds(1, TEAM - 1)], n, partner
        )
        if t == 0:
            pass_w.wait_recv()
        swap.wait_recv()

        def layer(rows):
            value = mm(look_in[t, 0, rows, :], w[0])
            for k in range(1, TEAM):
                value = value + mm(look_in[t, k, rows, :], w[k])
            return value

        def step(i, c):
            k = i + 1
            b = lax.rem(myb + k, nb)
            rows = pl.ds(pl.multiple_of(b * B, B), B)
            part_send[t, k] = layer(rows).astype(BF16)
            remote(part_send.at[t, k], part_recv.at[t, nb - k], n + 1, twin(k)).start()
            return c

        lax.fori_loop(0, nb - 1, step, 0)
        rows = pl.ds(pl.multiple_of(myb * B, B), B)
        pre = layer(rows) + bias[...]
        moved = remote(
            part_send.at[t, pl.ds(1, nb - 1)], part_recv.at[t, pl.ds(1, nb - 1)],
            n + 1, partner,
        )
        moved.wait_recv()
        for k in range(1, nb):
            pre = pre + part_recv[t, k].astype(F32)
        gate = jax.nn.sigmoid(pre)
        logits = jnp.sum(pre * gate * wout[...], axis=1, keepdims=True)
        return pre, gate, logits, [swap, moved]

    fetch(0, tabh, send_now, recv_now, 2)
    for blk in range(slots // 128):
        flipped = idcol[0, blk * 128 : (blk + 1) * 128, :].astype(F32).T
        idrow[:, blk * 128 : (blk + 1) * 128] = flipped[0:8, :].astype(jnp.int32)
    copy_w.wait_recv()
    pass_w.start()

    RC = 256

    def mark(i, c):
        rows = pl.ds(pl.multiple_of(i * RC, RC), RC)
        spot = lax.broadcasted_iota(jnp.int32, (RC, slots), 0) + i * RC
        scatter[rows, :] = onehot(idrow[0:1, :] == spot)
        return c

    lax.fori_loop(0, R // RC, mark, 0)
    copy_now = arrived(C, send_now, recv_now, 2)
    copy_now.wait_recv()
    pre, gate, logits, sent_now = forward(0, recv_now, 3)
    mine = pl.ds(pl.multiple_of(g * part + myb * B, B), B)
    error = jax.nn.sigmoid(logits) - colscr[mine, 2 * F : 2 * F + 1]
    slope[0] = (error * wout[...] * (gate * (1.0 + pre * (1.0 - gate)))).astype(BF16)

    def spread(k, c):
        remote(slope.at[0], slope.at[nb - k], 5, twin(k)).start()
        return c

    lax.fori_loop(1, nb, spread, 0)

    def back(k):
        rows = pl.ds(pl.multiple_of(lax.rem(myb + k, nb) * B, B), B)
        for side in range(TEAM):
            value = lax.dot_general(
                slope[k], w[side], (((1,), (1,)), ((), ())), preferred_element_type=F32
            ).astype(BF16)
            rg_out[side, rows, :] = value

    back(0)
    copy_slope = remote(slope.at[pl.ds(1, nb - 1)], slope.at[pl.ds(1, nb - 1)], 5, partner)
    copy_slope.wait_recv()
    for k in range(1, nb):
        back(k)
    for k in range(1, TEAM):
        remote(rg_out.at[k], rg.at[g], 6, mate(k)).start()
    rg[g] = rg_out[0]
    swap_grad = remote(
        rg_out.at[pl.ds(1, TEAM - 1)], rg.at[pl.ds(1, TEAM - 1)], 6, partner
    )
    swap_grad.wait_recv()
    grads = rg[...].reshape(S, FW)

    def give(i, c):
        rows = pl.ds(pl.multiple_of(i * GROUP, GROUP), GROUP)
        acc = jnp.zeros((GROUP, W), F32)
        spot = lax.broadcasted_iota(jnp.int32, (GROUP, S), 0) + i * GROUP
        for f in range(F):
            pick = onehot(rowscr[f : f + 1, :] == spot)
            acc = acc + mm(pick, grads[:, f * W : (f + 1) * W])
        send_grad[rows, :] = acc.astype(BF16)
        peers = GROUP // C
        exchange(C, send_grad, recv_grad, 7, jnp.maximum(i * peers, 1), (i + 1) * peers)
        return c

    lax.fori_loop(0, slots // GROUP, give, 0)
    recv_grad[0:C, :] = send_grad[0:C, :]
    loads[2].wait()
    loads[3].wait()
    copy_grad = arrived(C, send_grad, recv_grad, 7)
    copy_grad.wait_recv()

    gathered = jnp.concatenate([recv_grad[...], jnp.ones((slots, 128), BF16)], axis=1)

    def update(i, c):
        rows = pl.ds(pl.multiple_of(i * RC, RC), RC)
        both = mm(scatter[rows, :], gathered)
        grad, keep = both[:, :W], both[:, W:] > 0.5
        old_w, old_d, old_s = tab[rows, :], dual[rows, :], sq[rows, :]
        new_s = old_s + grad * grad
        root = jnp.sqrt(new_s)
        new_d = old_d + grad - (root - jnp.sqrt(old_s)) * old_w
        shrunk = jnp.where(new_d > 0.0, new_d - LASSO, new_d + LASSO)
        new_w = jnp.where(
            jnp.abs(new_d) <= LASSO, 0.0, -shrunk / ((BETA + root) + RIDGE)
        )
        new_w = jnp.where(keep, new_w, old_w)
        tab[rows, :] = new_w
        newh[rows, :] = new_w.astype(BF16)
        dual[rows, :] = jnp.where(keep, new_d, old_d)
        sq[rows, :] = jnp.where(keep, new_s, old_s)
        return c

    lax.fori_loop(0, R // RC, update, 0)
    stores = [
        pltpu.make_async_copy(tab, tab_o, osem.at[0]),
        pltpu.make_async_copy(dual, dual_o, osem.at[1]),
        pltpu.make_async_copy(sq, sq_o, osem.at[2]),
    ]
    for store in stores:
        store.start()

    fetch(1, newh, send_next, recv_next, 8)
    copy_next = arrived(C, send_next, recv_next, 8)
    copy_next.wait_recv()
    pre, gate, logits, sent_next = forward(1, recv_next, 9)
    lg_col[...] = jnp.zeros((128, 128), F32)
    lg_col[pl.ds(pl.multiple_of(myb * B, B), B), :] = jnp.broadcast_to(logits, (B, 128))
    lg_all[mp] = lg_col[...].T[0:8, :]

    def tell(k, c):
        remote(lg_all.at[mp], lg_all.at[mp], 11, (dp, lax.rem(mp + k, M))).start()
        return c

    lax.fori_loop(1, M, tell, 0)
    for copy in (copy_req, copy_w, pass_w, copy_now, *sent_now, copy_slope, swap_grad, copy_grad,
                 copy_next, *sent_next):
        copy.wait_send()
    for store in stores:
        store.wait()
    told = remote(lg_all.at[pl.ds(0, M - 1)], lg_all.at[pl.ds(0, M - 1)], 11, partner)
    told.wait_send()
    told.wait_recv()
    for k in range(TEAM):
        line = lg_all[k]
        for b in range(1, nb):
            line = line + lg_all[b * TEAM + k]
        lg_o[k : k + 1, :] = line[0:1, :]


def shards(table, dual, squares, now, later, labels, weight, bias, wout):
    M = lax.axis_size("mp")
    D = lax.axis_size("dp") * M
    R, W = table.shape
    S, F = now.shape
    H = weight.shape[1]
    C = 2 * now.size // D
    slots = D * C
    GROUP = 512
    part, nb, B = S // TEAM, M // TEAM, S // M
    vm = pl.BlockSpec(memory_space=pltpu.VMEM)
    hb = pl.BlockSpec(memory_space=pl.ANY)
    rows_buf = pltpu.VMEM((slots, W), BF16)
    big = pltpu.VMEM((R, W), F32)
    state = jax.ShapeDtypeStruct((R, W), F32)
    outs = pl.pallas_call(
        functools.partial(train, D, M, C, GROUP),
        out_shape=(state, state, state, jax.ShapeDtypeStruct((TEAM, 128), F32)),
        in_specs=[vm, vm, vm, vm, vm, hb, hb, hb, hb],
        out_specs=(hb, hb, hb, vm),
        scratch_shapes=[
            big, big, big,
            pltpu.VMEM((R, W), BF16), pltpu.VMEM((R, W), BF16),
            pltpu.VMEM((TEAM, F * W, H), BF16), pltpu.VMEM((R, slots), BF16),
            pltpu.VMEM((S, 128), F32), pltpu.VMEM((S, 128), jnp.int32),
            pltpu.VMEM((8, S), jnp.int32),
            pltpu.VMEM((D * 8, 128), jnp.int32), pltpu.VMEM((D * 8, 128), jnp.int32),
            pltpu.VMEM((2, slots, 128), jnp.int32), pltpu.VMEM((8, slots), jnp.int32),
            rows_buf, rows_buf, rows_buf, rows_buf, rows_buf, rows_buf,
            pltpu.VMEM((2, TEAM, part, F * W), BF16), pltpu.VMEM((2, TEAM, part, F * W), BF16),
            pltpu.VMEM((2, nb, B, H), BF16), pltpu.VMEM((2, nb, B, H), BF16),
            pltpu.VMEM((nb, B, H), BF16),
            pltpu.VMEM((TEAM, part, F * W), BF16), pltpu.VMEM((TEAM, part, F * W), BF16),
            pltpu.VMEM((128, 128), F32), pltpu.VMEM((M, 8, 128), F32),
            pltpu.SemaphoreType.DMA((4,)), pltpu.SemaphoreType.DMA((3,)),
            pltpu.SemaphoreType.DMA((13,)), pltpu.SemaphoreType.DMA((13,)),
        ],
        compiler_params=pltpu.CompilerParams(
            collective_id=0, has_side_effects=True, vmem_limit_bytes=58 * 1024 * 1024
        ),
    )(
        now.T, later.T, labels[None, :], bias[None, :], wout[None, :],
        table, dual, squares, weight,
    )
    logits = outs[3].reshape(S)
    return outs[0], outs[1], outs[2], logits


def solution(mesh):
    own = P(("dp", "mp"), None)
    placed = (own, own, own, P("dp", "mp"), P("dp", "mp"), P("dp"), P("mp", None), P(), P())
    return jax.shard_map(
        shards, mesh=mesh, in_specs=placed, out_specs=(own, own, own, P("dp")),
        check_vma=False,
    )
```

```python
import functools

import jax
import jax.numpy as jnp
from jax import lax
from jax.experimental import pallas as pl
from jax.experimental.pallas import tpu as pltpu
from jax.sharding import PartitionSpec as P

MESH = pl.DeviceIdType.MESH
LASSO = 0.1
RIDGE = 0.1
BETA = 1.0
TEAM = 4
F32 = jnp.float32
BF16 = jnp.bfloat16


def onehot(mask):
    return jnp.where(mask, 1.0, 0.0).astype(BF16)


def mm(a, b):
    return jnp.dot(a, b, preferred_element_type=F32)


def log2(v):
    assert v & (v - 1) == 0
    return v.bit_length() - 1


def train(
    D, M, C, GROUP,
    now_t, later_t, labels_t, bias, wout, table_h, dual_h, sq_h, w_h,
    tab_o, dual_o, sq_o, lg_o,
    tab, dual, sq, tabh, newh, w, scatter,
    colscr, slotcol, rowscr, req_send, asked, idcol, idrow,
    send_now, recv_now, send_grad, recv_grad, send_next, recv_next,
    look, look_in, part_send, part_recv, slope, rg, rg_out, lg_col, lg_all,
    lsem, osem, ssem, rsem,
):
    F, S = now_t.shape
    R, W = tab.shape
    H = bias.shape[1]
    FW = F * W
    part = S // TEAM
    nb = M // TEAM
    B = part // nb
    slots = D * C
    rsh, csh = log2(R), log2(C)
    dp, mp = lax.axis_index("dp"), lax.axis_index("mp")
    me = dp * M + mp
    g = lax.rem(mp, TEAM)
    myb = lax.div(mp, TEAM)
    core = lax.rem(dp, 2)
    side = lax.rem(lax.div(dp, 2), 2)
    sibling = (dp + 1 - 2 * core, mp)
    across = (dp + 2 - 4 * side, mp)

    def mate(k):
        return (dp, myb * TEAM + lax.rem(g + k, TEAM))

    def twin(k):
        return (dp, lax.rem(myb + k, nb) * TEAM + g)

    partner = mate(1)

    def device(p):
        return (lax.shift_right_logical(p, log2(M)), p & (M - 1))

    bar = pltpu.get_barrier_semaphore()

    def greet(k, c):
        pl.semaphore_signal(
            bar, inc=1, device_id=device((me + k) & (D - 1)), device_id_type=MESH
        )
        return c

    lax.fori_loop(1, D, greet, 0)

    loads = [
        pltpu.make_async_copy(table_h, tab, lsem.at[0]),
        pltpu.make_async_copy(w_h, w.at[0], lsem.at[1]),
        pltpu.make_async_copy(dual_h, dual, lsem.at[2]),
        pltpu.make_async_copy(sq_h, sq, lsem.at[3]),
    ]
    for load in loads:
        load.start()

    def remote(src, dst, n, to):
        return pltpu.make_async_remote_copy(
            src_ref=src, dst_ref=dst, send_sem=ssem.at[n], recv_sem=rsem.at[n],
            device_id=to, device_id_type=MESH,
        )

    lane = lax.broadcasted_iota(jnp.int32, (S, 128), 1)
    tri = onehot(
        lax.broadcasted_iota(jnp.int32, (S, S), 0)
        > lax.broadcasted_iota(jnp.int32, (S, S), 1)
    )
    sub = lax.broadcasted_iota(jnp.int32, (128, S), 0)
    stacked = jnp.zeros((128, S), F32)
    for q in range(2 * F + 1):
        line = labels_t[...] if q == 2 * F else (now_t, later_t)[q // F][q % F : q % F + 1, :]
        stacked = jnp.where(sub == q, line.astype(F32), stacked)
    colscr[...] = stacked.T
    cols = colscr[...].astype(jnp.int32)
    owners, members = [], []
    for q in range(2 * F):
        owner = (lax.shift_right_logical(cols[:, q : q + 1], rsh) - me) & (D - 1)
        owners.append(owner)
        members.append(jnp.where(owner == lane, 1.0, 0.0))
    counts = mm(tri, jnp.concatenate(members, axis=1).astype(BF16))
    ranks = []
    packed = jnp.zeros((S, 128), F32)
    for q in range(2 * F):
        count = counts[:, q * 128 : (q + 1) * 128]
        for before in range((q // F) * F, q):
            count = count + jnp.sum(members[before], axis=0, keepdims=True)
        rank = jnp.sum(count * members[q], axis=1, keepdims=True).astype(jnp.int32)
        ranks.append(rank)
        packed = jnp.where(lane == q, (owners[q] * C + rank).astype(F32), packed)
    slotcol[...] = packed.astype(jnp.int32)
    rowscr[...] = packed.T[0:8, :].astype(jnp.int32)
    total = jnp.zeros((D, 256), F32)
    owner_iota = lax.broadcasted_iota(jnp.int32, (D, S), 0)
    for q in range(2 * F):
        owner_row = lax.shift_right_logical(rowscr[q : q + 1, :], csh)
        which = ranks[q] + (q // F) * C == lane
        value = (cols[:, q : q + 1] & (R - 1)) + 1
        high = jnp.where(which, lax.shift_right_logical(value, 6).astype(F32), 0.0)
        low = jnp.where(which, (value & 63).astype(F32), 0.0)
        total += mm(
            onehot(owner_row == owner_iota),
            jnp.concatenate([high, low], axis=1).astype(BF16),
        )
    request = (total[:, :128] * 64.0 + total[:, 128:]).astype(jnp.int32) - 1
    for r in range(D):
        req_send[r * 8 : (r + 1) * 8, :] = jnp.broadcast_to(request[r : r + 1, :], (8, 128))

    pl.semaphore_wait(bar, D - 1)

    def exchange(rows, send, recv, n, first, last):
        def one(r, c):
            remote(
                send.at[pl.ds(pl.multiple_of(r * rows, rows), rows)],
                recv.at[pl.ds(pl.multiple_of((D - r) * rows, rows), rows)],
                n, device((me + r) & (D - 1)),
            ).start()
            return c

        lax.fori_loop(first, last, one, 0)

    def arrived(rows, send, recv, n):
        area = pl.ds(rows, (D - 1) * rows)
        return remote(send.at[area], recv.at[area], n, partner)

    exchange(8, req_send, asked, 0, 1, D)
    asked[0:8, :] = req_send[0:8, :]
    loads[1].wait()
    quarter = pl.ds(pl.multiple_of((2 * core + side) * (FW // 4), FW // 4), FW // 4)
    for k in range(1, TEAM):
        remote(w.at[0, quarter], w.at[TEAM - k, quarter], 1, mate(k)).start()
    share = w.at[pl.ds(1, TEAM - 1), quarter]
    copy_w = remote(share, share, 1, partner)
    cross_w = remote(share, share, 13, across)
    both = w.at[
        pl.ds(1, TEAM - 1), pl.ds(pl.multiple_of(core * (FW // 2), FW // 2), FW // 2)
    ]
    pass_w = remote(both, both, 12, sibling)
    loads[0].wait()
    tabh[...] = tab[...].astype(BF16)
    copy_req = arrived(8, req_send, asked, 0)
    copy_req.wait_recv()

    asked_t = asked[...].astype(F32).T.astype(jnp.int32)
    for r in range(D):
        for t in range(2):
            idcol[t, r * C : (r + 1) * C, :] = jnp.broadcast_to(
                asked_t[t * C : (t + 1) * C, 8 * r : 8 * r + 1], (C, 128)
            )

    KC = 1024

    def fetch(t, source, send, recv, n):
        def group(i, c):
            rows = pl.ds(pl.multiple_of(i * GROUP, GROUP), GROUP)
            ids = idcol[t, rows, 0:1]
            acc = jnp.zeros((GROUP, W), F32)
            for k in range(R // KC):
                pick = onehot(
                    ids == lax.broadcasted_iota(jnp.int32, (GROUP, KC), 1) + k * KC
                )
                acc = acc + mm(pick, source[k * KC : (k + 1) * KC, :])
            send[rows, :] = acc.astype(BF16)
            peers = GROUP // C
            exchange(C, send, recv, n, jnp.maximum(i * peers, 1), (i + 1) * peers)
            return c

        lax.fori_loop(0, slots // GROUP, group, 0)
        recv[0:C, :] = send[0:C, :]

    def forward(t, recv, n):
        def look_up(k):
            rows = pl.ds(pl.multiple_of(lax.rem(g + k, TEAM) * part, part), part)
            slot = jnp.concatenate(
                [slotcol[rows, t * F + f : t * F + f + 1] for f in range(F)], axis=0
            )
            pick = onehot(slot == lax.broadcasted_iota(jnp.int32, (F * part, slots), 1))
            got = mm(pick, recv[...]).astype(BF16)
            for f in range(F):
                look[t, k, :, f * W : (f + 1) * W] = got[f * part : (f + 1) * part]

        for k in range(1, TEAM):
            look_up(k)
            remote(look.at[t, k], look_in.at[t, TEAM - k], n, mate(k)).start()
        look_up(0)
        look_in[t, 0] = look[t, 0]
        swap = remote(
            look.at[t, pl.ds(1, TEAM - 1)], look_in.at[t, pl.ds(1, TEAM - 1)], n, partner
        )
        if t == 0:
            pass_w.wait_recv()
        swap.wait_recv()

        def layer(rows):
            value = mm(look_in[t, 0, rows, :], w[0])
            for k in range(1, TEAM):
                value = value + mm(look_in[t, k, rows, :], w[k])
            return value

        def step(i, c):
            k = i + 1
            b = lax.rem(myb + k, nb)
            rows = pl.ds(pl.multiple_of(b * B, B), B)
            part_send[t, k] = layer(rows).astype(BF16)
            remote(part_send.at[t, k], part_recv.at[t, nb - k], n + 1, twin(k)).start()
            return c

        lax.fori_loop(0, nb - 1, step, 0)
        rows = pl.ds(pl.multiple_of(myb * B, B), B)
        pre = layer(rows) + bias[...]
        moved = remote(
            part_send.at[t, pl.ds(1, nb - 1)], part_recv.at[t, pl.ds(1, nb - 1)],
            n + 1, partner,
        )
        moved.wait_recv()
        for k in range(1, nb):
            pre = pre + part_recv[t, k].astype(F32)
        gate = jax.nn.sigmoid(pre)
        logits = jnp.sum(pre * gate * wout[...], axis=1, keepdims=True)
        return pre, gate, logits, [swap, moved]

    copy_w.wait_recv()
    cross_w.start()
    fetch(0, tabh, send_now, recv_now, 2)
    for blk in range(slots // 128):
        flipped = idcol[0, blk * 128 : (blk + 1) * 128, :].astype(F32).T
        idrow[:, blk * 128 : (blk + 1) * 128] = flipped[0:8, :].astype(jnp.int32)
    cross_w.wait_recv()
    pass_w.start()

    RC = 1024

    def mark(i, c):
        rows = pl.ds(pl.multiple_of(i * RC, RC), RC)
        spot = lax.broadcasted_iota(jnp.int32, (RC, slots), 0) + i * RC
        scatter[rows, :] = onehot(idrow[0:1, :] == spot)
        return c

    lax.fori_loop(0, R // RC, mark, 0)
    copy_now = arrived(C, send_now, recv_now, 2)
    copy_now.wait_recv()
    pre, gate, logits, sent_now = forward(0, recv_now, 3)
    mine = pl.ds(pl.multiple_of(g * part + myb * B, B), B)
    error = jax.nn.sigmoid(logits) - colscr[mine, 2 * F : 2 * F + 1]
    slope[0] = (error * wout[...] * (gate * (1.0 + pre * (1.0 - gate)))).astype(BF16)

    def spread(k, c):
        remote(slope.at[0], slope.at[nb - k], 5, twin(k)).start()
        return c

    lax.fori_loop(1, nb, spread, 0)

    def back(k):
        rows = pl.ds(pl.multiple_of(lax.rem(myb + k, nb) * B, B), B)
        for side in range(TEAM):
            value = lax.dot_general(
                slope[k], w[side], (((1,), (1,)), ((), ())), preferred_element_type=F32
            ).astype(BF16)
            rg_out[side, rows, :] = value

    back(0)
    copy_slope = remote(slope.at[pl.ds(1, nb - 1)], slope.at[pl.ds(1, nb - 1)], 5, partner)
    copy_slope.wait_recv()
    for k in range(1, nb):
        back(k)
    for k in range(1, TEAM):
        remote(rg_out.at[k], rg.at[g], 6, mate(k)).start()
    rg[g] = rg_out[0]
    swap_grad = remote(
        rg_out.at[pl.ds(1, TEAM - 1)], rg.at[pl.ds(1, TEAM - 1)], 6, partner
    )
    swap_grad.wait_recv()
    grads = rg[...].reshape(S, FW)

    def give(i, c):
        rows = pl.ds(pl.multiple_of(i * GROUP, GROUP), GROUP)
        acc = jnp.zeros((GROUP, W), F32)
        spot = lax.broadcasted_iota(jnp.int32, (GROUP, S), 0) + i * GROUP
        for f in range(F):
            pick = onehot(rowscr[f : f + 1, :] == spot)
            acc = acc + mm(pick, grads[:, f * W : (f + 1) * W])
        send_grad[rows, :] = acc.astype(BF16)
        peers = GROUP // C
        exchange(C, send_grad, recv_grad, 7, jnp.maximum(i * peers, 1), (i + 1) * peers)
        return c

    lax.fori_loop(0, slots // GROUP, give, 0)
    recv_grad[0:C, :] = send_grad[0:C, :]
    loads[2].wait()
    loads[3].wait()
    copy_grad = arrived(C, send_grad, recv_grad, 7)
    copy_grad.wait_recv()

    gathered = jnp.concatenate([recv_grad[...], jnp.ones((slots, 128), BF16)], axis=1)

    def update(i, c):
        rows = pl.ds(pl.multiple_of(i * RC, RC), RC)
        both = mm(scatter[rows, :], gathered)
        grad, keep = both[:, :W], both[:, W:] > 0.5
        old_w, old_d, old_s = tab[rows, :], dual[rows, :], sq[rows, :]
        new_s = old_s + grad * grad
        root = jnp.sqrt(new_s)
        new_d = old_d + grad - (root - jnp.sqrt(old_s)) * old_w
        shrunk = jnp.where(new_d > 0.0, new_d - LASSO, new_d + LASSO)
        new_w = jnp.where(
            jnp.abs(new_d) <= LASSO, 0.0, -shrunk / ((BETA + root) + RIDGE)
        )
        new_w = jnp.where(keep, new_w, old_w)
        tab[rows, :] = new_w
        newh[rows, :] = new_w.astype(BF16)
        dual[rows, :] = jnp.where(keep, new_d, old_d)
        sq[rows, :] = jnp.where(keep, new_s, old_s)
        return c

    lax.fori_loop(0, R // RC, update, 0)
    stores = [
        pltpu.make_async_copy(tab, tab_o, osem.at[0]),
        pltpu.make_async_copy(dual, dual_o, osem.at[1]),
        pltpu.make_async_copy(sq, sq_o, osem.at[2]),
    ]
    for store in stores:
        store.start()

    fetch(1, newh, send_next, recv_next, 8)
    copy_next = arrived(C, send_next, recv_next, 8)
    copy_next.wait_recv()
    pre, gate, logits, sent_next = forward(1, recv_next, 9)
    lg_col[...] = jnp.zeros((128, 128), F32)
    lg_col[pl.ds(pl.multiple_of(myb * B, B), B), :] = jnp.broadcast_to(logits, (B, 128))
    lg_all[mp] = lg_col[...].T[0:8, :]

    def tell(k, c):
        remote(lg_all.at[mp], lg_all.at[mp], 11, (dp, lax.rem(mp + k, M))).start()
        return c

    lax.fori_loop(1, M, tell, 0)
    for copy in (copy_req, copy_w, cross_w, pass_w, copy_now, *sent_now, copy_slope, swap_grad, copy_grad,
                 copy_next, *sent_next):
        copy.wait_send()
    for store in stores:
        store.wait()
    told = remote(lg_all.at[pl.ds(0, M - 1)], lg_all.at[pl.ds(0, M - 1)], 11, partner)
    told.wait_send()
    told.wait_recv()
    for k in range(TEAM):
        line = lg_all[k]
        for b in range(1, nb):
            line = line + lg_all[b * TEAM + k]
        lg_o[k : k + 1, :] = line[0:1, :]


def shards(table, dual, squares, now, later, labels, weight, bias, wout):
    M = lax.axis_size("mp")
    D = lax.axis_size("dp") * M
    R, W = table.shape
    S, F = now.shape
    H = weight.shape[1]
    C = 2 * now.size // D
    slots = D * C
    GROUP = 256
    part, nb, B = S // TEAM, M // TEAM, S // M
    vm = pl.BlockSpec(memory_space=pltpu.VMEM)
    hb = pl.BlockSpec(memory_space=pl.ANY)
    rows_buf = pltpu.VMEM((slots, W), BF16)
    big = pltpu.VMEM((R, W), F32)
    state = jax.ShapeDtypeStruct((R, W), F32)
    outs = pl.pallas_call(
        functools.partial(train, D, M, C, GROUP),
        out_shape=(state, state, state, jax.ShapeDtypeStruct((TEAM, 128), F32)),
        in_specs=[vm, vm, vm, vm, vm, hb, hb, hb, hb],
        out_specs=(hb, hb, hb, vm),
        scratch_shapes=[
            big, big, big,
            pltpu.VMEM((R, W), BF16), pltpu.VMEM((R, W), BF16),
            pltpu.VMEM((TEAM, F * W, H), BF16), pltpu.VMEM((R, slots), BF16),
            pltpu.VMEM((S, 128), F32), pltpu.VMEM((S, 128), jnp.int32),
            pltpu.VMEM((8, S), jnp.int32),
            pltpu.VMEM((D * 8, 128), jnp.int32), pltpu.VMEM((D * 8, 128), jnp.int32),
            pltpu.VMEM((2, slots, 128), jnp.int32), pltpu.VMEM((8, slots), jnp.int32),
            rows_buf, rows_buf, rows_buf, rows_buf, rows_buf, rows_buf,
            pltpu.VMEM((2, TEAM, part, F * W), BF16), pltpu.VMEM((2, TEAM, part, F * W), BF16),
            pltpu.VMEM((2, nb, B, H), BF16), pltpu.VMEM((2, nb, B, H), BF16),
            pltpu.VMEM((nb, B, H), BF16),
            pltpu.VMEM((TEAM, part, F * W), BF16), pltpu.VMEM((TEAM, part, F * W), BF16),
            pltpu.VMEM((128, 128), F32), pltpu.VMEM((M, 8, 128), F32),
            pltpu.SemaphoreType.DMA((4,)), pltpu.SemaphoreType.DMA((3,)),
            pltpu.SemaphoreType.DMA((14,)), pltpu.SemaphoreType.DMA((14,)),
        ],
        compiler_params=pltpu.CompilerParams(
            collective_id=0, has_side_effects=True, vmem_limit_bytes=58 * 1024 * 1024
        ),
    )(
        now.T, later.T, labels[None, :], bias[None, :], wout[None, :],
        table, dual, squares, weight,
    )
    logits = outs[3].reshape(S)
    return outs[0], outs[1], outs[2], logits


def solution(mesh):
    own = P(("dp", "mp"), None)
    placed = (own, own, own, P("dp", "mp"), P("dp", "mp"), P("dp"), P("mp", None), P(), P())
    return jax.shard_map(
        shards, mesh=mesh, in_specs=placed, out_specs=(own, own, own, P("dp")),
        check_vma=False,
    )
```
